32 devices in a mesh: occ: 16 (over z, y, core), virt: 2 (over x).
Axes of the slice: x: 2, y: 2, z: 4, core: 2. Of those that a mesh axis runs over, the one named last changes fastest.
Arguments:
- factors_alpha: float32 [16, 512, 2048], P('occ', 'virt'), may hold values from -0.8 to 0.8
- factors_beta: float32 [16, 512, 2048], P('occ', 'virt'), may hold values from -0.8 to 0.8
- occ_energy: float32 [16], replicated, may hold values from -2.5 to -0.4
- vir_energy: float32 [512], replicated, may hold values from 0.3 to 3
- occ_orbital: int32 [16], replicated, may hold values from 0 to 15, each once
Outputs:
- grad_alpha: float32 [16, 512, 2048], P('occ', 'virt')
- grad_beta: float32 [16, 512, 2048], P('occ', 'virt')
The draws below stay inside these ranges and needn't reach their ends.
Inputs may be any that keep to these rules, and one draw needn't show every extreme that they name: `occ_orbital`: each index 0 .. 15 appears exactly once.
All inputs are finite; a program needn't handle non-finite values.
Results may differ from the reference program's by a relative error of at most 0.0003.
Values sent between devices are 32-bit elements; how exact they have to be, the bound alone decides.
A program may use at most 64 MiB of HBM per device.

```python
import jax
import jax.numpy as jnp
from jax import lax

NV = 512
NAUX = 2048
OCC_DEV = 1
REACH = 3
NOCC = 16


def shard_levels(stream_key, shape, split, least, top_value):
    def one(position, parts):
        steps = jax.random.uniform(jax.random.fold_in(jax.random.fold_in(stream_key, 6), position), (parts,), jnp.float32, least / len(split), top_value / len(split))
        return jnp.repeat(jnp.exp(steps), shape[position] // parts).reshape((-1,) + (1,) * (len(shape) - position - 1))

    level = one(*split[0])
    for cut in split[1:]:
        level = level * one(*cut)
    return level


def noise(rng, dims, width, bound, pieces=(), kind=jnp.bfloat16):
    gain = shard_levels(rng, dims, pieces, -0.22, 0.18) if pieces else 1.0
    result = jax.random.normal(rng, dims, jnp.float32) * width * gain
    return jnp.minimum(jnp.maximum(result, -bound), bound).astype(kind)


def setup_inputs(seed: int = 0) -> dict:
    seeds = jax.random.split(jax.random.key(seed), 6)
    factors_alpha = noise(seeds[0], (NOCC, NV, NAUX), 0.1, 0.8, ((0, 16), (1, 2)), jnp.float32)
    factors_beta = noise(seeds[1], (NOCC, NV, NAUX), 0.1, 0.8, ((0, 16), (1, 2)), jnp.float32)
    occ_energy = jnp.clip(jax.random.uniform(seeds[2], (NOCC,), jnp.float32, -2.5, -0.4), -2.5, -0.4)
    vir_energy = jnp.clip(jax.random.uniform(seeds[3], (NV,), jnp.float32, 0.3, 3.0), 0.3, 3.0)
    occ_orbital = jax.random.permutation(seeds[4], NOCC).astype(jnp.int32)
    return {"factors_alpha": factors_alpha, "factors_beta": factors_beta, "occ_energy": occ_energy, "vir_energy": vir_energy, "occ_orbital": occ_orbital}


def reference(factors_alpha, factors_beta, occ_energy, vir_energy, occ_orbital):
    e_occ = occ_energy[occ_orbital]
    groups = NOCC // OCC_DEV
    alpha_groups = factors_alpha.reshape(groups, OCC_DEV, NV, NAUX)
    beta_groups = factors_beta.reshape(groups, OCC_DEV, NV, NAUX)
    energy_groups = e_occ.reshape(groups, OCC_DEV)
    high = lax.Precision.HIGHEST

    def amplitudes(g, h):
        integrals = jnp.einsum("iap,jbp->iajb", alpha_groups[g], beta_groups[h], precision=high)
        denom = (energy_groups[g][:, None, None, None] - vir_energy[None, :, None, None]
                 + energy_groups[h][None, None, :, None] - vir_energy[None, None, None, :])
        return integrals / denom

    def alpha_side(g):
        total = jnp.zeros((OCC_DEV, NV, NAUX), jnp.float32)
        for offset in range(-REACH, REACH + 1):
            h = ((g + offset) % groups).astype(jnp.int32)
            total = total + jnp.einsum("iajb,jbp->iap", amplitudes(g, h), beta_groups[h], precision=high)
        return total

    def beta_side(h):
        total = jnp.zeros((OCC_DEV, NV, NAUX), jnp.float32)
        for offset in range(-REACH, REACH + 1):
            g = ((h + offset) % groups).astype(jnp.int32)
            total = total + jnp.einsum("iajb,iap->jbp", amplitudes(g, h), alpha_groups[g], precision=high)
        return total

    order = jnp.arange(groups, dtype=jnp.int32)
    grad_alpha = lax.map(alpha_side, order).reshape(NOCC, NV, NAUX)
    grad_beta = lax.map(beta_side, order).reshape(NOCC, NV, NAUX)
    return grad_alpha, grad_beta
```

```python
import jax
import jax.numpy as jnp
from jax import lax
from jax.sharding import PartitionSpec as P

REACH = 3


def shards(factors_alpha, factors_beta, occ_energy, vir_energy, occ_orbital):
    high = lax.Precision.HIGH
    vir_dev = factors_alpha.shape[1]
    n_groups = lax.axis_size("occ")
    n_slabs = lax.axis_size("virt")
    here = lax.axis_index("occ")
    slab_index = lax.axis_index("virt")
    side = 1 - 2 * (here % 2)

    def swap(value):
        return lax.ppermute(value, "occ", [(i, i ^ 1) for i in range(n_groups)])

    def outward(value):
        return lax.ppermute(
            value, "occ", [(i, (i + 2 - 4 * (i % 2)) % n_groups) for i in range(n_groups)]
        )

    def inward(value):
        return lax.ppermute(
            value, "occ", [(i, (i - 2 + 4 * (i % 2)) % n_groups) for i in range(n_groups)]
        )

    def far(value):
        return lax.ppermute(
            value, "occ", [(i, (i - 3 + 6 * (i % 2)) % n_groups) for i in range(n_groups)]
        )

    own = factors_beta[0]
    slabs = {0: own}
    slabs[2] = inward(own)
    slabs[-2] = outward(own)
    slabs[-3] = far(own)
    slabs[1] = swap(own)
    slabs[-1] = swap(slabs[2])
    slabs[3] = swap(slabs[-2])
    whole_alpha = lax.all_gather(factors_alpha[0], "virt", axis=0, tiled=True)

    total_occ = occ_orbital.shape[0]
    picks = (occ_orbital[:, None] == jnp.arange(total_occ, dtype=jnp.int32)[None, :]).astype(
        jnp.float32
    )
    orbital_energy = jnp.dot(picks, occ_energy, precision=lax.Precision.HIGHEST)
    own_energy = lax.dynamic_index_in_dim(orbital_energy, here, keepdims=False)
    vir_local = lax.dynamic_slice_in_dim(vir_energy, slab_index * vir_dev, vir_dev)
    base = own_energy - vir_energy[:, None]

    def amplitudes(offset):
        group = (here + side * offset + n_groups) % n_groups
        pair_energy = lax.dynamic_index_in_dim(orbital_energy, group, keepdims=False)
        integrals = jnp.einsum("ap,bp->ab", whole_alpha, slabs[offset], precision=high)
        return integrals / (base + pair_energy - vir_local[None, :])

    def beta_term(amps):
        return jnp.einsum("ab,ap->bp", amps, whole_alpha, precision=high)

    amps = {}
    terms = {}
    for offset in (0, 1, -3, -2, 2, 3, -1):
        amps[offset] = amplitudes(offset)
        terms[offset] = beta_term(amps[offset])

    from_far = far(terms[-3])
    from_partner = swap(terms[1])
    from_behind = outward(terms[2] + swap(terms[-1]))
    from_ahead = inward(terms[-2] + swap(terms[3]))
    grad_beta = terms[0] + from_partner + from_far + from_behind + from_ahead

    order = (0, 1, -3, -2, 2, 3, -1)

    def alpha_rows(slab):
        total = None
        for offset in order:
            rows = lax.dynamic_slice_in_dim(amps[offset], slab * vir_dev, vir_dev)
            term = jnp.einsum("ab,bp->ap", rows, slabs[offset], precision=high)
            total = term if total is None else total + term
        return total

    arrived = []
    for shift in range(1, n_slabs):
        part = alpha_rows((slab_index + shift) % n_slabs)
        arrived.append(
            lax.ppermute(part, "virt", [(v, (v + shift) % n_slabs) for v in range(n_slabs)])
        )
    grad_alpha = alpha_rows(slab_index)
    for part in arrived:
        grad_alpha = grad_alpha + part
    return (grad_alpha[None], grad_beta[None])


def solution(mesh):
    return jax.shard_map(
        shards,
        mesh=mesh,
        in_specs=(P("occ", "virt", None), P("occ", "virt", None), P(), P(), P()),
        out_specs=(P("occ", "virt", None), P("occ", "virt", None)),
        check_vma=False,
    )
```

```python
import jax
import jax.numpy as jnp
from jax import lax
from jax.sharding import PartitionSpec as P

REACH = 3


def shards(factors_alpha, factors_beta, occ_energy, vir_energy, occ_orbital):
    high = lax.Precision.HIGH
    vir_dev = factors_alpha.shape[1]
    n_groups = lax.axis_size("occ")
    n_slabs = lax.axis_size("virt")
    here = lax.axis_index("occ")
    slab_index = lax.axis_index("virt")
    side = 1 - 2 * (here % 2)

    def swap(value):
        return lax.ppermute(value, "occ", [(i, i ^ 1) for i in range(n_groups)])

    def outward(value):
        return lax.ppermute(
            value, "occ", [(i, (i + 2 - 4 * (i % 2)) % n_groups) for i in range(n_groups)]
        )

    def inward(value):
        return lax.ppermute(
            value, "occ", [(i, (i - 2 + 4 * (i % 2)) % n_groups) for i in range(n_groups)]
        )

    def far(value):
        return lax.ppermute(
            value, "occ", [(i, (i - 3 + 6 * (i % 2)) % n_groups) for i in range(n_groups)]
        )

    own = factors_beta[0]
    slabs = {0: own}
    slabs[1] = swap(own)
    slabs[-3] = far(own)
    slabs[2] = inward(own)
    slabs[-2] = outward(own)
    whole_alpha = lax.all_gather(factors_alpha[0], "virt", axis=0, tiled=True)

    total_occ = occ_orbital.shape[0]
    picks = (occ_orbital[:, None] == jnp.arange(total_occ, dtype=jnp.int32)[None, :]).astype(
        jnp.float32
    )
    orbital_energy = jnp.dot(picks, occ_energy, precision=lax.Precision.HIGHEST)
    own_energy = lax.dynamic_index_in_dim(orbital_energy, here, keepdims=False)
    vir_local = lax.dynamic_slice_in_dim(vir_energy, slab_index * vir_dev, vir_dev)
    base = own_energy - vir_energy[:, None]

    def amplitudes(offset):
        group = (here + side * offset + n_groups) % n_groups
        pair_energy = lax.dynamic_index_in_dim(orbital_energy, group, keepdims=False)
        integrals = jnp.einsum("ap,bp->ab", whole_alpha, slabs[offset], precision=high)
        return integrals / (base + pair_energy - vir_local[None, :])

    def beta_term(amps):
        return jnp.einsum("ab,ap->bp", amps, whole_alpha, precision=high)

    def alpha_rows(slab, offsets, total):
        for offset in offsets:
            rows = lax.dynamic_slice_in_dim(amps[offset], slab * vir_dev, vir_dev)
            term = jnp.einsum("ab,bp->ap", rows, slabs[offset], precision=high)
            total = term if total is None else total + term
        return total

    shifts = range(1, n_slabs)
    amps = {}
    terms = {}
    near = (0, 1, -3)
    for offset in near:
        amps[offset] = amplitudes(offset)
        terms[offset] = beta_term(amps[offset])
    given = [alpha_rows((slab_index + shift) % n_slabs, near, None) for shift in shifts]
    slabs[2], slabs[-2], terms, given = lax.optimization_barrier(
        (slabs[2], slabs[-2], terms, given)
    )
    from_far = far(terms[-3])
    from_partner = swap(terms[1])

    slabs[-1] = swap(slabs[2])
    slabs[3] = swap(slabs[-2])
    for offset in (2, -2, -1, 3):
        amps[offset] = amplitudes(offset)
        terms[offset] = beta_term(amps[offset])
    to_outward = terms[2] + swap(terms[-1])
    to_inward = terms[-2] + swap(terms[3])
    to_outward, to_inward, amps, given = lax.optimization_barrier(
        (to_outward, to_inward, amps, given)
    )
    from_behind = outward(to_outward)
    from_ahead = inward(to_inward)

    rest = (2, -2, -1, 3)
    arrived = []
    for shift, start in zip(shifts, given):
        part = alpha_rows((slab_index + shift) % n_slabs, rest, start)
        arrived.append(
            lax.ppermute(part, "virt", [(v, (v + shift) % n_slabs) for v in range(n_slabs)])
        )
    grad_alpha = alpha_rows(slab_index, near + rest, None)
    for part in arrived:
        grad_alpha = grad_alpha + part
    grad_beta = terms[0] + from_partner + from_far + from_behind + from_ahead
    return (grad_alpha[None], grad_beta[None])


def solution(mesh):
    return jax.shard_map(
        shards,
        mesh=mesh,
        in_specs=(P("occ", "virt", None), P("occ", "virt", None), P(), P(), P()),
        out_specs=(P("occ", "virt", None), P("occ", "virt", None)),
        check_vma=False,
    )
```

```python
import jax
import jax.numpy as jnp
from jax import lax
from jax.sharding import PartitionSpec as P

REACH = 3


def shards(factors_alpha, factors_beta, occ_energy, vir_energy, occ_orbital):
    high = lax.Precision.HIGH
    vir_dev = factors_alpha.shape[1]
    n_groups = lax.axis_size("occ")
    n_slabs = lax.axis_size("virt")
    here = lax.axis_index("occ")
    slab_index = lax.axis_index("virt")
    side = 1 - 2 * (here % 2)

    def swap(value):
        return lax.ppermute(value, "occ", [(i, i ^ 1) for i in range(n_groups)])

    def outward(value):
        return lax.ppermute(
            value, "occ", [(i, (i + 2 - 4 * (i % 2)) % n_groups) for i in range(n_groups)]
        )

    def inward(value):
        return lax.ppermute(
            value, "occ", [(i, (i - 2 + 4 * (i % 2)) % n_groups) for i in range(n_groups)]
        )

    def far(value):
        return lax.ppermute(
            value, "occ", [(i, (i - 3 + 6 * (i % 2)) % n_groups) for i in range(n_groups)]
        )

    own = factors_beta[0]
    slabs = {0: own}
    slabs[1] = swap(own)
    slabs[-3] = far(own)
    slabs[2] = inward(own)
    slabs[-2] = outward(own)
    whole_alpha = lax.all_gather(factors_alpha[0], "virt", axis=0, tiled=True)

    total_occ = occ_orbital.shape[0]
    picks = (occ_orbital[:, None] == jnp.arange(total_occ, dtype=jnp.int32)[None, :]).astype(
        jnp.float32
    )
    orbital_energy = jnp.dot(picks, occ_energy, precision=lax.Precision.HIGHEST)
    own_energy = lax.dynamic_index_in_dim(orbital_energy, here, keepdims=False)
    vir_local = lax.dynamic_slice_in_dim(vir_energy, slab_index * vir_dev, vir_dev)
    base = own_energy - vir_energy[:, None]

    def amplitudes(offset):
        group = (here + side * offset + n_groups) % n_groups
        pair_energy = lax.dynamic_index_in_dim(orbital_energy, group, keepdims=False)
        integrals = jnp.einsum("ap,bp->ab", whole_alpha, slabs[offset], precision=high)
        return integrals / (base + pair_energy - vir_local[None, :])

    def beta_term(amps):
        return jnp.einsum("ab,ap->bp", amps, whole_alpha, precision=high)

    def alpha_rows(slab, offsets, total):
        for offset in offsets:
            rows = lax.dynamic_slice_in_dim(amps[offset], slab * vir_dev, vir_dev)
            term = jnp.einsum("ab,bp->ap", rows, slabs[offset], precision=high)
            total = term if total is None else total + term
        return total

    shifts = range(1, n_slabs)
    amps = {}
    terms = {}
    near = (0, 1, -3)
    for offset in near:
        amps[offset] = amplitudes(offset)
        terms[offset] = beta_term(amps[offset])
    given = [alpha_rows((slab_index + shift) % n_slabs, near, None) for shift in shifts]
    slabs[2], slabs[-2], terms, given = lax.optimization_barrier(
        (slabs[2], slabs[-2], terms, given)
    )
    slabs[-1] = swap(slabs[2])
    slabs[3] = swap(slabs[-2])
    for offset in (2, -2, -1, 3):
        amps[offset] = amplitudes(offset)
        terms[offset] = beta_term(amps[offset])
    to_outward = terms[2] + swap(terms[-1])
    to_inward = terms[-2] + swap(terms[3])
    to_outward, to_inward, amps, given, terms = lax.optimization_barrier(
        (to_outward, to_inward, amps, given, terms)
    )
    from_behind = outward(to_outward)
    from_ahead = inward(to_inward)
    from_far = far(terms[-3])
    from_partner = swap(terms[1])

    rest = (2, -2, -1, 3)
    arrived = []
    for shift, start in zip(shifts, given):
        part = alpha_rows((slab_index + shift) % n_slabs, rest, start)
        arrived.append(
            lax.ppermute(part, "virt", [(v, (v + shift) % n_slabs) for v in range(n_slabs)])
        )
    grad_alpha = alpha_rows(slab_index, near + rest, None)
    for part in arrived:
        grad_alpha = grad_alpha + part
    grad_beta = terms[0] + from_partner + from_far + from_behind + from_ahead
    return (grad_alpha[None], grad_beta[None])


def solution(mesh):
    return jax.shard_map(
        shards,
        mesh=mesh,
        in_specs=(P("occ", "virt", None), P("occ", "virt", None), P(), P(), P()),
        out_specs=(P("occ", "virt", None), P("occ", "virt", None)),
        check_vma=False,
    )
```
